1024 devices in a mesh: region: 128 (over y_lo, x, z), group: 8 (over y_hi, core).
Axes of the slice: x: 8, y: 8 (y_hi: 4, y_lo: 2; y = y_hi * 2 + y_lo), z: 8, core: 2. Of those that a mesh axis runs over, the one named last changes fastest.
Arguments:
- observations: bfloat16 [81, 4194304], P(None, ('region', 'group')), may hold values from -13 to 13
- obs_index: int32 [16384, 2048], P(('region', 'group')), may hold values from 0 to 8191
- obs_count: int32 [16384], P(('region', 'group')), may hold values from 0 to 2048, as said below
- localization: float32 [16384, 2048], P(('region', 'group')), may hold values from 0.1 to 1
- background: bfloat16 [16384, 80, 512], P(('region', 'group')), may hold values from -6 to 6
- background_mean: float32 [16384, 512], P(('region', 'group')), may hold values from -6 to 6
Outputs:
- analysis: bfloat16 [16384, 80, 512], P(('region', 'group'))
The draws below stay inside these ranges and needn't reach their ends.
Inputs may be any that keep to these rules, and one draw needn't show every extreme that they name: `obs_count`: A block has either no local observations (count 0) or at least 256 of them; most devices own some blocks without observations, and some device has all its blocks observed.
All inputs are finite; a program needn't handle non-finite values.
Results may differ from the reference program's by a relative error of at most 0.0027.
Values may be sent and summed in bfloat16 or wider, within the bound.
No kernel may reach another device: no remote copies, remote signals or barrier semaphores. Data moves between devices by JAX's collectives and lax.ppermute only.
A program may use at most 32 MiB of HBM per device.

```python
import math
import jax
import jax.numpy as jnp
from jax import lax

MEMBERS = 80
ROWS = 81
CELLS = 512
BLK_DEV = 16
P_MAX = 2048
OBS_DEV = 4096
HALO = 2048
NS_ITERS = 6
BLOCKS = 16384
OBS = 4194304
N_REGION = 128
N_GROUP = 8


def draw_obs_count(key, part):
    devices = BLOCKS // BLK_DEV
    key_active, key_full, key_order, key_size = jax.random.split(key, 4)
    active_blocks = jax.random.randint(key_active, (devices, 1), 0, BLK_DEV + 1)
    full_device = jax.random.randint(key_full, (), 0, devices)
    device_ids = jnp.arange(devices, dtype=jnp.int32)[:, None]
    active_blocks = jnp.where(device_ids == full_device, BLK_DEV, active_blocks)
    scores = jax.random.randint(key_order, (devices, BLK_DEV), 0, 2 ** 20) * BLK_DEV + jnp.arange(BLK_DEV, dtype=jnp.int32)[None, :]
    ranking = jnp.argsort(jnp.argsort(scores, axis=1), axis=1)
    counts = jax.random.randint(key_size, (devices, BLK_DEV), P_MAX // 8, P_MAX + 1)
    counts = jnp.where(ranking < active_blocks, counts, 0)
    counts = jnp.where((device_ids == full_device) & (ranking == 0), P_MAX, counts)
    return counts.reshape(BLOCKS).astype(jnp.int32)


def draw_observations(key, part):
    key_noise, key_amp, key_dir, key_inn = jax.random.split(jax.random.fold_in(key, 17), 4)
    noise = jnp.clip(jax.random.normal(key_noise, (MEMBERS, OBS), jnp.float32), -4.0, 4.0)
    amplitude = jnp.clip(jax.random.normal(key_amp, (1, OBS), jnp.float32), -3.0, 3.0)
    innovation = jnp.clip(jax.random.normal(key_inn, (1, OBS), jnp.float32), -4.0, 4.0)
    direction = jnp.clip(jax.random.normal(key_dir, (MEMBERS, 1), jnp.float32), -3.0, 3.0)
    member_rows = noise + amplitude * direction
    return jnp.concatenate([member_rows, innovation], axis=0).astype(jnp.bfloat16)


def set_ends(drawn, own_key, smallest, largest):
    dims = drawn.shape
    index_at = [jax.random.randint(jax.random.fold_in(own_key, axis), (), 0, dims[axis]) for axis in range(len(dims))]
    drawn = drawn.at[tuple(index_at)].set(smallest)
    longest = dims.index(max(dims))
    index_at[longest] = (index_at[longest] + 1) % dims[longest]
    return drawn.at[tuple(index_at)].set(largest)


def levels(rng, extent, shards, low, largest):
    factor_of = 1.0
    for axis_at, parts in shards:
        draws = jax.random.uniform(jax.random.fold_in(jax.random.fold_in(rng, 6), axis_at), (parts,), jnp.float32, low / len(shards), largest / len(shards))
        factor_of = factor_of * jnp.repeat(jnp.exp(draws), extent[axis_at] // parts).reshape((-1,) + (1,) * (len(extent) - 1 - axis_at))
    return factor_of


def bell_draw(stream_key, extent, scale, bound, shards=(), held_as=jnp.bfloat16):
    loudness = levels(stream_key, extent, shards, -0.22, 0.18) if shards else 1.0
    array = jax.random.normal(stream_key, extent, jnp.float32) * scale * loudness
    return jnp.minimum(jnp.maximum(array, -bound), bound).astype(held_as)


def setup_inputs(seed: int = 0) -> dict:
    seeds = jax.random.split(jax.random.key(seed), 7)
    return {
        "observations": draw_observations(jax.random.fold_in(seeds[6], 71), 0),
        "obs_index": set_ends(jax.random.randint(seeds[1], (BLOCKS, P_MAX), 0, OBS_DEV + 2 * HALO), jax.random.fold_in(seeds[1], 1), 0, (OBS_DEV + 2 * HALO) - 1).astype(jnp.int32),
        "obs_count": draw_obs_count(jax.random.fold_in(seeds[6], 71), 0),
        "localization": jnp.clip(0.1 + 0.9 * jax.random.uniform(seeds[3], (BLOCKS, P_MAX), jnp.float32) ** levels(seeds[3], (BLOCKS, P_MAX), ((0, 1024),), -0.2, 0.2), 0.1, 1.0),
        "background": bell_draw(seeds[4], (BLOCKS, MEMBERS, CELLS), 1.0, 6.0, ((0, 1024),)),
        "background_mean": bell_draw(seeds[5], (BLOCKS, CELLS), 1.0, 6.0, ((0, 1024),), jnp.float32),
    }


def matmul_high(left, right):
    return jnp.einsum('nij,njk->nik', left, right, precision=lax.Precision.HIGHEST)

def solve_weights(gram):
    members = gram.shape[1] - 1
    identity = jnp.eye(members, dtype=jnp.float32)
    information = gram[:, :members, :members] + (members - 1.0) * identity
    innovation_term = gram[:, :members, members]
    scale = jnp.sqrt(lax.optimization_barrier(jnp.sum(information * information, axis=(1, 2))))
    iterate_y = information / scale[:, None, None]
    iterate_z = jnp.broadcast_to(identity, information.shape)
    for sweep in range(NS_ITERS):
        factor = 1.5 * identity - 0.5 * matmul_high(iterate_z, iterate_y)
        iterate_y = matmul_high(iterate_y, factor)
        iterate_z = matmul_high(factor, iterate_z)
    spread_part = math.sqrt(members - 1.0) * iterate_z / jnp.sqrt(scale)[:, None, None]
    covariance = matmul_high(iterate_z, iterate_z) / scale[:, None, None]
    mean_shift = jnp.einsum('nij,nj->ni', covariance, innovation_term, precision=lax.Precision.HIGHEST)
    return spread_part + mean_shift[:, :, None]

def reference(observations, obs_index, obs_count, localization, background, background_mean):
    devices = N_REGION * N_GROUP
    per_device = observations.reshape(ROWS, devices, OBS_DEV)
    identity = jnp.eye(MEMBERS, dtype=jnp.float32)

    def one_device(device):
        region = device // N_GROUP
        member = device % N_GROUP
        lower = (region - 1) % N_REGION * N_GROUP + member
        upper = (region + 1) % N_REGION * N_GROUP + member
        lower_rows = lax.dynamic_index_in_dim(per_device, lower, axis=1, keepdims=False)
        own_rows = lax.dynamic_index_in_dim(per_device, device, axis=1, keepdims=False)
        upper_rows = lax.dynamic_index_in_dim(per_device, upper, axis=1, keepdims=False)
        extended = jnp.concatenate([lower_rows[:, OBS_DEV - HALO:], own_rows, upper_rows[:, :HALO]], axis=1)
        first = (device * BLK_DEV).astype(jnp.int32)
        indices = lax.dynamic_slice_in_dim(obs_index, first, BLK_DEV, 0).astype(jnp.int32)
        counts = lax.dynamic_slice_in_dim(obs_count, first, BLK_DEV, 0)
        factors = lax.dynamic_slice_in_dim(localization, first, BLK_DEV, 0)
        states = lax.dynamic_slice_in_dim(background, first, BLK_DEV, 0)
        means = lax.dynamic_slice_in_dim(background_mean, first, BLK_DEV, 0)
        within = (jnp.arange(P_MAX, dtype=jnp.int32)[None, :] < counts[:, None]).astype(factors.dtype)
        extended_wide = extended.astype(jnp.float32)
        local = jnp.take(extended_wide, indices, axis=1)
        weighted = (local * (factors * within)[None]).astype(jnp.bfloat16)
        gram = jnp.einsum('kbp,lbp->bkl', weighted.astype(jnp.float32), local)
        solved = solve_weights(gram)
        weights = jnp.where((counts > 0)[:, None, None], solved, identity).astype(jnp.bfloat16)
        mixed = jnp.einsum('bji,bjr->bir', weights.astype(jnp.float32), states.astype(jnp.float32))
        return (means[:, None, :] + mixed).astype(jnp.bfloat16)
    result = lax.map(one_device, jnp.arange(devices, dtype=jnp.int32))
    return result.reshape(BLOCKS, MEMBERS, CELLS)
```

```python
import functools
import math

import jax
import jax.numpy as jnp
from jax import lax
from jax.experimental import pallas as pl
from jax.experimental.pallas import tpu as pltpu
from jax.sharding import PartitionSpec as P

HALO = 2048
NS_ITERS = 6
LANES = 128
BF16 = jnp.bfloat16
F32 = jnp.float32
NT = (((1,), (1,)), ((), ()))

hist_unroll = 2
gram_chunk = 8
solve_batch = 4


def histogram(block, count_ref, index_ref, factor_ref, w_ref):
    blocks, p_most = index_ref.shape
    groups = w_ref.shape[0] // blocks
    index = index_ref[pl.ds(block, 1), :]
    factor = factor_ref[pl.ds(block, 1), :]
    place = lax.broadcasted_iota(jnp.int32, (1, p_most), 1)
    factor = jnp.where(place < count_ref[block], factor, 0.0)
    hi = lax.shift_right_logical(index, 7)
    lo = lax.bitwise_and(index, LANES - 1)
    hi_at = lax.broadcasted_iota(jnp.int32, (groups, p_most), 0)
    lo_at = lax.broadcasted_iota(jnp.int32, (LANES, p_most), 0)
    hi_hot = jnp.where(hi_at == hi, factor, 0.0).astype(BF16)
    lo_hot = jnp.where(lo_at == lo, 1.0, 0.0).astype(BF16)
    summed = lax.dot_general(hi_hot, lo_hot, NT, preferred_element_type=F32)
    w_ref[pl.ds(block, groups, stride=blocks), :] = summed


def gram_part(record, w_ref, first, blocks):
    members = record.shape[0] - 1
    pieces = []
    for j in range(record.shape[1] // LANES):
        columns = slice(j * LANES, (j + 1) * LANES)
        perturbations = record[:members, columns]
        innovation = record[members:, columns].astype(F32)
        w = w_ref[pl.ds(pl.multiple_of((first + j) * blocks, blocks), blocks), :]
        rows = []
        for b in range(blocks):
            w_b = jnp.broadcast_to(w[b : b + 1, :], (16, LANES)).astype(BF16)
            rows.append(perturbations * jnp.concatenate([w_b] * (members // 16), axis=0))
        rows.append(w.astype(BF16) * jnp.broadcast_to(innovation, (blocks, LANES)).astype(BF16))
        pieces.append(jnp.concatenate(rows, axis=0))
    weighted = jnp.concatenate(pieces, axis=1)
    return lax.dot_general(weighted, record[:members], NT, preferred_element_type=F32)


def add_gram(record_ref, w_ref, first, blocks, sum_ref):
    width = gram_chunk * LANES

    def step(c, carry):
        record = record_ref[:, pl.ds(pl.multiple_of(c * width, width), width)]
        sum_ref[...] += gram_part(record, w_ref, first + c * gram_chunk, blocks)
        return carry

    lax.fori_loop(0, record_ref.shape[1] // width, step, 0)


def own_gram_kernel(count_ref, index_ref, factor_ref, record_ref, gram_ref, w_ref):
    blocks = index_ref.shape[0]

    def step(i, carry):
        for j in range(hist_unroll):
            histogram(i * hist_unroll + j, count_ref, index_ref, factor_ref, w_ref)
        return carry

    lax.fori_loop(0, blocks // hist_unroll, step, 0)
    gram_ref[...] = jnp.zeros_like(gram_ref)
    add_gram(record_ref, w_ref, HALO // LANES, blocks, gram_ref)


def own_gram(obs_count, obs_index, localization, record):
    blocks, p_most = obs_index.shape
    rows, columns = record.shape
    groups = (columns + 2 * HALO) // LANES
    vmem = pl.BlockSpec(memory_space=pltpu.VMEM)
    return pl.pallas_call(
        own_gram_kernel,
        out_shape=(
            jax.ShapeDtypeStruct((blocks * rows, rows - 1), F32),
            jax.ShapeDtypeStruct((groups * blocks, LANES), F32),
        ),
        in_specs=[pl.BlockSpec(memory_space=pltpu.SMEM), vmem, vmem, vmem],
        out_specs=(vmem, vmem),
        compiler_params=pltpu.CompilerParams(vmem_limit_bytes=40 * 2**20),
        cost_estimate=pl.CostEstimate(
            flops=8_000_000_000, bytes_accessed=8_000_000, transcendentals=0
        ),
        name="own_gram",
    )(obs_count, obs_index, localization, record)


def three(x):
    return jnp.concatenate([x, x, x], axis=1)


def left_terms(x):
    third = x.shape[1] // 3
    lane = lax.broadcasted_iota(jnp.int32, x.shape, 1)
    middle = (lane >= third) & (lane < 2 * third)
    return jnp.where(middle, x - x.astype(BF16).astype(F32), x).astype(BF16)


def right_terms(x):
    upper = x.astype(BF16)
    lower = (x - upper.astype(F32)).astype(BF16)
    return jnp.concatenate([upper, upper, lower], axis=0)


def solve_blocks(informations, innovations):
    members = informations[0].shape[0]
    row_at = lax.broadcasted_iota(jnp.int32, (members, members), 0)
    column_at = lax.broadcasted_iota(jnp.int32, (members, members), 1)
    eye = (row_at == column_at).astype(F32)
    eye_3 = three(eye)
    s, z, t, squares = [], [], [], []
    for gram, innovation in zip(informations, innovations):
        information = gram + (members - 1.0) * eye
        square = jnp.sum(information * information, axis=1, keepdims=True)
        square = jnp.sum(square, axis=0, keepdims=True)
        squares.append(square)
        s.append(three(information * lax.rsqrt(square)))
        t.append(jnp.broadcast_to(three(innovation), (8, 3 * members)))
        z.append(None)
    for sweep in range(NS_ITERS):
        final = sweep == NS_ITERS - 1
        rights = [right_terms(x) for x in s]
        for i in range(len(s)):
            lefts = ([] if final else [s[i]]) + ([z[i]] if sweep else []) + [t[i]]
            product = jnp.dot(
                left_terms(jnp.concatenate(lefts, axis=0)), rights[i], preferred_element_type=F32
            )
            at = 0 if final else members
            if sweep:
                z[i] = 1.5 * z[i] - 0.5 * product[at : at + members]
            else:
                z[i] = 1.5 * eye_3 - 0.5 * s[i]
            if not final:
                s[i] = 1.5 * s[i] - 0.5 * product[:members]
            t[i] = 1.5 * t[i] - 0.5 * product[-8:]
        for i in range(len(s)):
            lefts = ([] if final else [s[i]]) + [t[i]]
            product = jnp.dot(
                left_terms(jnp.concatenate(lefts, axis=0)), rights[i], preferred_element_type=F32
            )
            if not final:
                s[i] = 1.5 * s[i] - 0.5 * product[:members]
            t[i] = 1.5 * t[i] - 0.5 * product[-8:]
    solved = []
    for square, z_i, t_i in zip(squares, z, t):
        inverse = lax.rsqrt(square)
        spread = (math.sqrt(members - 1.0) * jnp.sqrt(inverse)) * z_i[:, :members]
        solved.append(spread + inverse * t_i[:1, :members])
    return solved, eye


def finish_kernel(
    count_ref, own_ref, w_ref, lower_ref, upper_ref, background_ref, mean_ref, out_ref, gram_ref
):
    step = pl.program_id(0)
    blocks = count_ref.shape[0]
    members = background_ref.shape[1]

    @pl.when(step == 0)
    def _():
        gram_ref[...] = own_ref[...]
        groups = w_ref.shape[0] // blocks
        add_gram(lower_ref, w_ref, 0, blocks, gram_ref)
        add_gram(upper_ref, w_ref, groups - HALO // LANES, blocks, gram_ref)

    informations, innovations = [], []
    for i in range(solve_batch):
        b = step * solve_batch + i
        informations.append(gram_ref[pl.ds(pl.multiple_of(b * members, members), members), :])
        innovations.append(gram_ref[pl.ds(blocks * members + b, 1), :])
    solved, eye = solve_blocks(informations, innovations)
    for i in range(solve_batch):
        b = step * solve_batch + i
        weights = jnp.where(count_ref[b] > 0, solved[i], eye).astype(BF16)
        mixed = jnp.dot(weights, background_ref[i], preferred_element_type=F32)
        out_ref[i] = (mean_ref[pl.ds(b, 1), :] + mixed).astype(BF16)


def finish(obs_count, own, w, lower, upper, background, background_mean):
    blocks, members, cells = background.shape

    def whole(x):
        return pl.BlockSpec(x.shape, lambda i: (0,) * x.ndim)

    states = pl.BlockSpec((solve_batch, members, cells), lambda i: (i, 0, 0))
    return pl.pallas_call(
        finish_kernel,
        grid=(blocks // solve_batch,),
        out_shape=jax.ShapeDtypeStruct(background.shape, BF16),
        in_specs=[
            pl.BlockSpec(memory_space=pltpu.SMEM),
            whole(own),
            whole(w),
            whole(lower),
            whole(upper),
            states,
            whole(background_mean),
        ],
        out_specs=states,
        scratch_shapes=[pltpu.VMEM(own.shape, F32)],
        compiler_params=pltpu.CompilerParams(vmem_limit_bytes=40 * 2**20),
        name="finish",
    )(obs_count, own, w, lower, upper, background, background_mean)


def on_device(observations, obs_index, obs_count, localization, background, background_mean):
    count = lax.axis_size("region")
    up = [(i, (i + 1) % count) for i in range(count)]
    down = [(j, i) for i, j in up]
    own_columns = observations.shape[1]
    lower = lax.ppermute(observations[:, own_columns - HALO :], "region", up)
    upper = lax.ppermute(observations[:, :HALO], "region", down)
    own, w = own_gram(obs_count, obs_index, localization, observations)
    return finish(obs_count, own, w, lower, upper, background, background_mean)


def solution(mesh):
    return jax.shard_map(
        on_device,
        mesh=mesh,
        in_specs=(
            P(None, ("region", "group")),
            P(("region", "group"), None),
            P(("region", "group")),
            P(("region", "group"), None),
            P(("region", "group"), None, None),
            P(("region", "group"), None),
        ),
        out_specs=P(("region", "group"), None, None),
        check_vma=False,
    )
```

```python
import functools
import math

import jax
import jax.numpy as jnp
from jax import lax
from jax.experimental import pallas as pl
from jax.experimental.pallas import tpu as pltpu
from jax.sharding import PartitionSpec as P

HALO = 2048
NS_ITERS = 6
RUN = 8
LANES = 128
BF16 = jnp.bfloat16
F32 = jnp.float32
NT = (((1,), (1,)), ((), ()))

hist_unroll = 2
gram_chunk = 8
solve_batch = 8


def histogram(block, count_ref, index_ref, factor_ref, w_ref):
    blocks, p_most = index_ref.shape
    groups = w_ref.shape[0] // blocks
    index = index_ref[pl.ds(block, 1), :]
    factor = factor_ref[pl.ds(block, 1), :]
    place = lax.broadcasted_iota(jnp.int32, (1, p_most), 1)
    factor = jnp.where(place < count_ref[block], factor, 0.0)
    hi = lax.shift_right_logical(index, 7)
    lo = lax.bitwise_and(index, LANES - 1)
    hi_at = lax.broadcasted_iota(jnp.int32, (groups, p_most), 0)
    lo_at = lax.broadcasted_iota(jnp.int32, (LANES, p_most), 0)
    hi_hot = jnp.where(hi_at == hi, factor, 0.0).astype(BF16)
    lo_hot = jnp.where(lo_at == lo, 1.0, 0.0).astype(BF16)
    summed = lax.dot_general(hi_hot, lo_hot, NT, preferred_element_type=F32)
    w_ref[pl.ds(block, groups, stride=blocks), :] = summed


def gram_part(record, w_ref, first, blocks):
    members = record.shape[0] - 1
    pieces = []
    for j in range(record.shape[1] // LANES):
        columns = slice(j * LANES, (j + 1) * LANES)
        perturbations = record[:members, columns]
        innovation = record[members:, columns].astype(F32)
        w = w_ref[pl.ds(pl.multiple_of((first + j) * blocks, blocks), blocks), :]
        rows = []
        for b in range(blocks):
            w_b = jnp.broadcast_to(w[b : b + 1, :], (16, LANES)).astype(BF16)
            rows.append(perturbations * jnp.concatenate([w_b] * (members // 16), axis=0))
        rows.append(w.astype(BF16) * jnp.broadcast_to(innovation, (blocks, LANES)).astype(BF16))
        pieces.append(jnp.concatenate(rows, axis=0))
    weighted = jnp.concatenate(pieces, axis=1)
    return lax.dot_general(weighted, record[:members], NT, preferred_element_type=F32)


def add_gram(record_ref, w_ref, first, blocks, sum_ref):
    width = gram_chunk * LANES

    def step(c, carry):
        record = record_ref[:, pl.ds(pl.multiple_of(c * width, width), width)]
        sum_ref[...] += gram_part(record, w_ref, first + c * gram_chunk, blocks)
        return carry

    lax.fori_loop(0, record_ref.shape[1] // width, step, 0)


def own_gram_body(count_ref, index_ref, factor_ref, record_ref, gram_ref, w_ref):
    blocks = index_ref.shape[0]

    def step(i, carry):
        for j in range(hist_unroll):
            histogram(i * hist_unroll + j, count_ref, index_ref, factor_ref, w_ref)
        return carry

    lax.fori_loop(0, blocks // hist_unroll, step, 0)
    gram_ref[...] = jnp.zeros_like(gram_ref)
    add_gram(record_ref, w_ref, HALO // LANES, blocks, gram_ref)


def first_turn_kernel(turn_ref, *refs):
    @pl.when(turn_ref[0] == 0)
    def _():
        own_gram_body(*refs)


def second_turn_kernel(turn_ref, count, index, factor, record, gram_in, w_in, gram_ref, w_ref):
    del gram_in, w_in

    @pl.when(turn_ref[0] != 0)
    def _():
        own_gram_body(count, index, factor, record, gram_ref, w_ref)


def own_gram(turn, obs_count, obs_index, localization, record, made=()):
    blocks, p_most = obs_index.shape
    rows, columns = record.shape
    groups = (columns + 2 * HALO) // LANES
    smem = pl.BlockSpec(memory_space=pltpu.SMEM)
    vmem = pl.BlockSpec(memory_space=pltpu.VMEM)
    return pl.pallas_call(
        second_turn_kernel if made else first_turn_kernel,
        out_shape=(
            jax.ShapeDtypeStruct((blocks * rows, rows - 1), F32),
            jax.ShapeDtypeStruct((groups * blocks, LANES), F32),
        ),
        in_specs=[smem, smem, vmem, vmem, vmem] + [vmem] * len(made),
        out_specs=(vmem, vmem),
        input_output_aliases={5: 0, 6: 1} if made else {},
        compiler_params=pltpu.CompilerParams(vmem_limit_bytes=40 * 2**20),
        cost_estimate=pl.CostEstimate(
            flops=8_000_000_000, bytes_accessed=8_000_000, transcendentals=0
        ),
        name="own_gram_second" if made else "own_gram_first",
    )(turn, obs_count, obs_index, localization, record, *made)


def upper_gram_kernel(gram_in, w_ref, upper_ref, gram_ref):
    blocks = gram_in.shape[0] // upper_ref.shape[0]
    groups = w_ref.shape[0] // blocks
    gram_ref[...] = gram_in[...]
    add_gram(upper_ref, w_ref, groups - HALO // LANES, blocks, gram_ref)


def upper_gram(own, w, upper):
    vmem = pl.BlockSpec(memory_space=pltpu.VMEM)
    return pl.pallas_call(
        upper_gram_kernel,
        out_shape=jax.ShapeDtypeStruct(own.shape, F32),
        in_specs=[vmem, vmem, vmem],
        out_specs=vmem,
        input_output_aliases={0: 0},
        compiler_params=pltpu.CompilerParams(vmem_limit_bytes=40 * 2**20),
        cost_estimate=pl.CostEstimate(
            flops=2_000_000_000, bytes_accessed=2_000_000, transcendentals=0
        ),
        name="upper_gram",
    )(own, w, upper)


def padded(x):
    return jnp.concatenate([x, jnp.zeros((x.shape[0], LANES - x.shape[1]), x.dtype)], axis=1)


def terms(x):
    upper = x.astype(BF16)
    return upper, (x - upper.astype(F32)).astype(BF16)


def right_terms(x):
    upper, lower = terms(x)
    rest = jnp.zeros((LANES - x.shape[0], LANES), BF16)
    return (
        jnp.concatenate([upper, rest, upper, rest], axis=0),
        jnp.concatenate([lower, rest], axis=0),
    )


def multiply(x, right):
    upper, lower = terms(x)
    return jnp.dot(
        jnp.concatenate([upper, lower], axis=1), right[0], preferred_element_type=F32
    ) + jnp.dot(upper, right[1], preferred_element_type=F32)


def solve_blocks(informations, innovations):
    members = informations[0].shape[0]
    row_at = lax.broadcasted_iota(jnp.int32, (members, LANES), 0)
    column_at = lax.broadcasted_iota(jnp.int32, (members, LANES), 1)
    eye = (row_at == column_at).astype(F32)
    s, z, t, squares = [], [], [], []
    for gram, innovation in zip(informations, innovations):
        information = padded(gram) + (members - 1.0) * eye
        square = jnp.sum(information * information, axis=1, keepdims=True)
        square = jnp.sum(square, axis=0, keepdims=True)
        squares.append(square)
        s.append(information * lax.rsqrt(square))
        t.append(jnp.broadcast_to(padded(innovation), (8, LANES)))
        z.append(None)
    for sweep in range(NS_ITERS):
        final = sweep == NS_ITERS - 1
        rights = [right_terms(x) for x in s]
        for i in range(len(s)):
            lefts = ([] if final else [s[i]]) + ([z[i]] if sweep else []) + [t[i]]
            product = multiply(jnp.concatenate(lefts, axis=0), rights[i])
            at = 0 if final else members
            if sweep:
                z[i] = 1.5 * z[i] - 0.5 * product[at : at + members]
            else:
                z[i] = 1.5 * eye - 0.5 * s[i]
            if not final:
                s[i] = 1.5 * s[i] - 0.5 * product[:members]
            t[i] = 1.5 * t[i] - 0.5 * product[-8:]
        for i in range(len(s)):
            lefts = ([] if final else [s[i]]) + [t[i]]
            product = multiply(jnp.concatenate(lefts, axis=0), rights[i])
            if not final:
                s[i] = 1.5 * s[i] - 0.5 * product[:members]
            t[i] = 1.5 * t[i] - 0.5 * product[-8:]
    solved = []
    for square, z_i, t_i in zip(squares, z, t):
        inverse = lax.rsqrt(square)
        spread = (math.sqrt(members - 1.0) * jnp.sqrt(inverse)) * z_i[:, :members]
        solved.append(spread + inverse * t_i[:1, :members])
    return solved, eye[:, :members]


def finish_kernel(
    count_ref, own_ref, w_ref, lower_ref, background_ref, mean_ref, out_ref, gram_ref
):
    step = pl.program_id(0)
    blocks = count_ref.shape[0]
    members = background_ref.shape[1]

    @pl.when(step == 0)
    def _():
        gram_ref[...] = own_ref[...]
        add_gram(lower_ref, w_ref, 0, blocks, gram_ref)

    informations, innovations = [], []
    for i in range(solve_batch):
        b = step * solve_batch + i
        informations.append(gram_ref[pl.ds(pl.multiple_of(b * members, members), members), :])
        innovations.append(gram_ref[pl.ds(blocks * members + b, 1), :])
    solved, eye = solve_blocks(informations, innovations)
    for i in range(solve_batch):
        b = step * solve_batch + i
        weights = jnp.where(count_ref[b] > 0, solved[i], eye).astype(BF16)
        mixed = jnp.dot(weights, background_ref[i], preferred_element_type=F32)
        out_ref[i] = (mean_ref[pl.ds(b, 1), :] + mixed).astype(BF16)


def finish(obs_count, own, w, lower, background, background_mean):
    blocks, members, cells = background.shape

    def whole(x):
        return pl.BlockSpec(x.shape, lambda i: (0,) * x.ndim)

    states = pl.BlockSpec((solve_batch, members, cells), lambda i: (i, 0, 0))
    return pl.pallas_call(
        finish_kernel,
        grid=(blocks // solve_batch,),
        out_shape=jax.ShapeDtypeStruct(background.shape, BF16),
        in_specs=[
            pl.BlockSpec(memory_space=pltpu.SMEM),
            whole(own),
            whole(w),
            whole(lower),
            states,
            whole(background_mean),
        ],
        out_specs=states,
        scratch_shapes=[pltpu.VMEM(own.shape, F32)],
        compiler_params=pltpu.CompilerParams(vmem_limit_bytes=40 * 2**20),
        name="finish",
    )(obs_count, own, w, lower, background, background_mean)


def on_device(observations, obs_index, obs_count, localization, background, background_mean):
    count = lax.axis_size("region")
    up = [(i, (i + 1) % count) for i in range(count)]
    down = [(j, i) for i, j in up]
    own_columns = observations.shape[1]
    place = lax.axis_index("region")
    turn = jnp.minimum(place % RUN, 1).astype(jnp.int32)[None]
    given = (turn, obs_count, obs_index, localization, observations)
    lower = lax.ppermute(observations[:, own_columns - HALO :], "region", up)
    made = own_gram(*given)
    after, *made = lax.optimization_barrier((observations, *made))
    upper = lax.ppermute(after[:, :HALO], "region", down)
    own, w = own_gram(*given, made)
    own = upper_gram(own, w, upper)
    return finish(obs_count, own, w, lower, background, background_mean)


def solution(mesh):
    return jax.shard_map(
        on_device,
        mesh=mesh,
        in_specs=(
            P(None, ("region", "group")),
            P(("region", "group"), None),
            P(("region", "group")),
            P(("region", "group"), None),
            P(("region", "group"), None, None),
            P(("region", "group"), None),
        ),
        out_specs=P(("region", "group"), None, None),
        check_vma=False,
    )
```

```python
import functools
import math

import jax
import jax.numpy as jnp
from jax import lax
from jax.experimental import pallas as pl
from jax.experimental.pallas import tpu as pltpu
from jax.sharding import PartitionSpec as P

HALO = 2048
NS_ITERS = 6
LANES = 128
BF16 = jnp.bfloat16
F32 = jnp.float32
NT = (((1,), (1,)), ((), ()))

hist_unroll = 2
gram_chunk = 8
solve_batch = 8


def histogram(block, count_ref, index_ref, factor_ref, w_ref):
    blocks, p_most = index_ref.shape
    groups = w_ref.shape[0] // blocks
    index = index_ref[pl.ds(block, 1), :]
    factor = factor_ref[pl.ds(block, 1), :]
    place = lax.broadcasted_iota(jnp.int32, (1, p_most), 1)
    factor = jnp.where(place < count_ref[block], factor, 0.0)
    hi = lax.shift_right_logical(index, 7)
    lo = lax.bitwise_and(index, LANES - 1)
    hi_at = lax.broadcasted_iota(jnp.int32, (groups, p_most), 0)
    lo_at = lax.broadcasted_iota(jnp.int32, (LANES, p_most), 0)
    hi_hot = jnp.where(hi_at == hi, factor, 0.0).astype(BF16)
    lo_hot = jnp.where(lo_at == lo, 1.0, 0.0).astype(BF16)
    summed = lax.dot_general(hi_hot, lo_hot, NT, preferred_element_type=F32)
    w_ref[pl.ds(block, groups, stride=blocks), :] = summed


def gram_part(record, w_ref, first, blocks):
    members = record.shape[0] - 1
    pieces = []
    for j in range(record.shape[1] // LANES):
        columns = slice(j * LANES, (j + 1) * LANES)
        perturbations = record[:members, columns]
        innovation = record[members:, columns].astype(F32)
        w = w_ref[pl.ds(pl.multiple_of((first + j) * blocks, blocks), blocks), :]
        rows = []
        for b in range(blocks):
            w_b = jnp.broadcast_to(w[b : b + 1, :], (16, LANES)).astype(BF16)
            rows.append(perturbations * jnp.concatenate([w_b] * (members // 16), axis=0))
        rows.append(w.astype(BF16) * jnp.broadcast_to(innovation, (blocks, LANES)).astype(BF16))
        pieces.append(jnp.concatenate(rows, axis=0))
    weighted = jnp.concatenate(pieces, axis=1)
    return lax.dot_general(weighted, record[:members], NT, preferred_element_type=F32)


def add_gram(record_ref, w_ref, first, blocks, sum_ref):
    width = gram_chunk * LANES

    def step(c, carry):
        record = record_ref[:, pl.ds(pl.multiple_of(c * width, width), width)]
        sum_ref[...] += gram_part(record, w_ref, first + c * gram_chunk, blocks)
        return carry

    lax.fori_loop(0, record_ref.shape[1] // width, step, 0)


def own_gram_kernel(count_ref, index_ref, factor_ref, record_ref, gram_ref, w_ref):
    blocks = index_ref.shape[0]

    def step(i, carry):
        for j in range(hist_unroll):
            histogram(i * hist_unroll + j, count_ref, index_ref, factor_ref, w_ref)
        return carry

    lax.fori_loop(0, blocks // hist_unroll, step, 0)
    gram_ref[...] = jnp.zeros_like(gram_ref)
    add_gram(record_ref, w_ref, HALO // LANES, blocks, gram_ref)


def own_gram(obs_count, obs_index, localization, record):
    blocks, p_most = obs_index.shape
    rows, columns = record.shape
    groups = (columns + 2 * HALO) // LANES
    smem = pl.BlockSpec(memory_space=pltpu.SMEM)
    vmem = pl.BlockSpec(memory_space=pltpu.VMEM)
    return pl.pallas_call(
        own_gram_kernel,
        out_shape=(
            jax.ShapeDtypeStruct((blocks * rows, rows - 1), F32),
            jax.ShapeDtypeStruct((groups * blocks, LANES), F32),
        ),
        in_specs=[smem, vmem, vmem, vmem],
        out_specs=(vmem, vmem),
        compiler_params=pltpu.CompilerParams(vmem_limit_bytes=40 * 2**20),
        cost_estimate=pl.CostEstimate(
            flops=8_000_000_000, bytes_accessed=8_000_000, transcendentals=0
        ),
        name="own_gram",
    )(obs_count, obs_index, localization, record)


def padded(x):
    return jnp.concatenate([x, jnp.zeros((x.shape[0], LANES - x.shape[1]), x.dtype)], axis=1)


def terms(x):
    upper = x.astype(BF16)
    return upper, (x - upper.astype(F32)).astype(BF16)


def right_terms(x):
    upper, lower = terms(x)
    rest = jnp.zeros((LANES - x.shape[0], LANES), BF16)
    return (
        jnp.concatenate([upper, rest, upper, rest], axis=0),
        jnp.concatenate([lower, rest], axis=0),
    )


def multiply(x, right):
    upper, lower = terms(x)
    return jnp.dot(
        jnp.concatenate([upper, lower], axis=1), right[0], preferred_element_type=F32
    ) + jnp.dot(upper, right[1], preferred_element_type=F32)


def solve_blocks(informations, innovations):
    members = informations[0].shape[0]
    row_at = lax.broadcasted_iota(jnp.int32, (members, LANES), 0)
    column_at = lax.broadcasted_iota(jnp.int32, (members, LANES), 1)
    eye = (row_at == column_at).astype(F32)
    s, z, t, squares = [], [], [], []
    for gram, innovation in zip(informations, innovations):
        information = padded(gram) + (members - 1.0) * eye
        square = jnp.sum(information * information, axis=1, keepdims=True)
        square = jnp.sum(square, axis=0, keepdims=True)
        squares.append(square)
        s.append(information * lax.rsqrt(square))
        t.append(jnp.broadcast_to(padded(innovation), (8, LANES)))
        z.append(None)
    for sweep in range(NS_ITERS):
        final = sweep == NS_ITERS - 1
        rights = [right_terms(x) for x in s]
        for i in range(len(s)):
            lefts = ([] if final else [s[i]]) + ([z[i]] if sweep else []) + [t[i]]
            product = multiply(jnp.concatenate(lefts, axis=0), rights[i])
            at = 0 if final else members
            if sweep:
                z[i] = 1.5 * z[i] - 0.5 * product[at : at + members]
            else:
                z[i] = 1.5 * eye - 0.5 * s[i]
            if not final:
                s[i] = 1.5 * s[i] - 0.5 * product[:members]
            t[i] = 1.5 * t[i] - 0.5 * product[-8:]
        for i in range(len(s)):
            lefts = ([] if final else [s[i]]) + [t[i]]
            product = multiply(jnp.concatenate(lefts, axis=0), rights[i])
            if not final:
                s[i] = 1.5 * s[i] - 0.5 * product[:members]
            t[i] = 1.5 * t[i] - 0.5 * product[-8:]
    solved = []
    for square, z_i, t_i in zip(squares, z, t):
        inverse = lax.rsqrt(square)
        spread = (math.sqrt(members - 1.0) * jnp.sqrt(inverse)) * z_i[:, :members]
        solved.append(spread + inverse * t_i[:1, :members])
    return solved, eye[:, :members]


def finish_kernel(
    count_ref,
    odd_ref,
    own_ref,
    w_ref,
    far_ref,
    near_ref,
    background_ref,
    mean_ref,
    out_ref,
    gram_ref,
):
    step = pl.program_id(0)
    blocks = count_ref.shape[0]
    members = background_ref.shape[1]

    @pl.when(step == 0)
    def _():
        gram_ref[...] = own_ref[...]
        upper = w_ref.shape[0] // blocks - HALO // LANES
        odd = odd_ref[0]
        add_gram(near_ref, w_ref, odd * upper, blocks, gram_ref)
        add_gram(far_ref, w_ref, (1 - odd) * upper, blocks, gram_ref)

    informations, innovations = [], []
    for i in range(solve_batch):
        b = step * solve_batch + i
        informations.append(gram_ref[pl.ds(pl.multiple_of(b * members, members), members), :])
        innovations.append(gram_ref[pl.ds(blocks * members + b, 1), :])
    solved, eye = solve_blocks(informations, innovations)
    for i in range(solve_batch):
        b = step * solve_batch + i
        weights = jnp.where(count_ref[b] > 0, solved[i], eye).astype(BF16)
        mixed = jnp.dot(weights, background_ref[i], preferred_element_type=F32)
        out_ref[i] = (mean_ref[pl.ds(b, 1), :] + mixed).astype(BF16)


def finish(obs_count, odd, own, w, far, near, background, background_mean):
    blocks, members, cells = background.shape

    def whole(x):
        return pl.BlockSpec(x.shape, lambda i: (0,) * x.ndim)

    states = pl.BlockSpec((solve_batch, members, cells), lambda i: (i, 0, 0))
    return pl.pallas_call(
        finish_kernel,
        grid=(blocks // solve_batch,),
        out_shape=jax.ShapeDtypeStruct(background.shape, BF16),
        in_specs=[
            pl.BlockSpec(memory_space=pltpu.SMEM),
            pl.BlockSpec(memory_space=pltpu.SMEM),
            whole(own),
            whole(w),
            whole(far),
            whole(near),
            states,
            whole(background_mean),
        ],
        out_specs=states,
        scratch_shapes=[pltpu.VMEM(own.shape, F32)],
        compiler_params=pltpu.CompilerParams(vmem_limit_bytes=40 * 2**20),
        name="finish",
    )(obs_count, odd, own, w, far, near, background, background_mean)


def on_device(observations, obs_index, obs_count, localization, background, background_mean):
    count = lax.axis_size("region")
    odd = lax.axis_index("region") % 2

    def swap(record, parity):
        below = record[:, :HALO]
        above = record[:, record.shape[1] - HALO :]
        sent = jnp.where(odd == parity, above, below)
        pairs = [((2 * i + parity) % count, (2 * i + 1 + parity) % count) for i in range(count // 2)]
        pairs += [(j, i) for i, j in pairs]
        return sent, pairs

    sent_1, pairs_1 = swap(observations, 1)
    sent_2, pairs_2 = swap(observations, 0)
    far = lax.ppermute(sent_2, "region", pairs_2)
    near = lax.ppermute(sent_1, "region", pairs_1)
    own, w = own_gram(obs_count, obs_index, localization, observations)
    odd = odd.astype(jnp.int32)[None]
    return finish(obs_count, odd, own, w, far, near, background, background_mean)


def solution(mesh):
    return jax.shard_map(
        on_device,
        mesh=mesh,
        in_specs=(
            P(None, ("region", "group")),
            P(("region", "group"), None),
            P(("region", "group")),
            P(("region", "group"), None),
            P(("region", "group"), None, None),
            P(("region", "group"), None),
        ),
        out_specs=P(("region", "group"), None, None),
        check_vma=False,
    )
```

```python
import functools
import math

import jax
import jax.numpy as jnp
from jax import lax
from jax.experimental import pallas as pl
from jax.experimental.pallas import tpu as pltpu
from jax.sharding import PartitionSpec as P

HALO = 2048
NS_ITERS = 6
RUN = 8
LANES = 128
BF16 = jnp.bfloat16
F32 = jnp.float32
NT = (((1,), (1,)), ((), ()))

hist_unroll = 2
gram_chunk = 8
solve_batch = 8


def histogram(block, count_ref, index_ref, factor_ref, w_ref):
    blocks, p_most = index_ref.shape
    groups = w_ref.shape[0] // blocks
    index = index_ref[pl.ds(block, 1), :]
    factor = factor_ref[pl.ds(block, 1), :]
    place = lax.broadcasted_iota(jnp.int32, (1, p_most), 1)
    factor = jnp.where(place < count_ref[block], factor, 0.0)
    hi = lax.shift_right_logical(index, 7)
    lo = lax.bitwise_and(index, LANES - 1)
    hi_at = lax.broadcasted_iota(jnp.int32, (groups, p_most), 0)
    lo_at = lax.broadcasted_iota(jnp.int32, (LANES, p_most), 0)
    hi_hot = jnp.where(hi_at == hi, factor, 0.0).astype(BF16)
    lo_hot = jnp.where(lo_at == lo, 1.0, 0.0).astype(BF16)
    summed = lax.dot_general(hi_hot, lo_hot, NT, preferred_element_type=F32)
    w_ref[pl.ds(block, groups, stride=blocks), :] = summed


def gram_part(record, w_ref, first, blocks):
    members = record.shape[0] - 1
    pieces = []
    for j in range(record.shape[1] // LANES):
        columns = slice(j * LANES, (j + 1) * LANES)
        perturbations = record[:members, columns]
        innovation = record[members:, columns].astype(F32)
        w = w_ref[pl.ds(pl.multiple_of((first + j) * blocks, blocks), blocks), :]
        rows = []
        for b in range(blocks):
            w_b = jnp.broadcast_to(w[b : b + 1, :], (16, LANES)).astype(BF16)
            rows.append(perturbations * jnp.concatenate([w_b] * (members // 16), axis=0))
        rows.append(w.astype(BF16) * jnp.broadcast_to(innovation, (blocks, LANES)).astype(BF16))
        pieces.append(jnp.concatenate(rows, axis=0))
    weighted = jnp.concatenate(pieces, axis=1)
    return lax.dot_general(weighted, record[:members], NT, preferred_element_type=F32)


def add_gram(record_ref, w_ref, first, blocks, sum_ref):
    width = gram_chunk * LANES

    def step(c, carry):
        record = record_ref[:, pl.ds(pl.multiple_of(c * width, width), width)]
        sum_ref[...] += gram_part(record, w_ref, first + c * gram_chunk, blocks)
        return carry

    lax.fori_loop(0, record_ref.shape[1] // width, step, 0)


def own_gram_body(count_ref, index_ref, factor_ref, record_ref, gram_ref, w_ref):
    blocks = index_ref.shape[0]

    def step(i, carry):
        for j in range(hist_unroll):
            histogram(i * hist_unroll + j, count_ref, index_ref, factor_ref, w_ref)
        return carry

    lax.fori_loop(0, blocks // hist_unroll, step, 0)
    gram_ref[...] = jnp.zeros_like(gram_ref)
    add_gram(record_ref, w_ref, HALO // LANES, blocks, gram_ref)


def first_turn_kernel(turn_ref, *refs):
    @pl.when(turn_ref[0] == 0)
    def _():
        own_gram_body(*refs)


def second_turn_kernel(turn_ref, count, index, factor, record, gram_in, w_in, gram_ref, w_ref):
    del gram_in, w_in

    @pl.when(turn_ref[0] != 0)
    def _():
        own_gram_body(count, index, factor, record, gram_ref, w_ref)


def own_gram(turn, obs_count, obs_index, localization, record, made=()):
    blocks, p_most = obs_index.shape
    rows, columns = record.shape
    groups = (columns + 2 * HALO) // LANES
    smem = pl.BlockSpec(memory_space=pltpu.SMEM)
    vmem = pl.BlockSpec(memory_space=pltpu.VMEM)
    return pl.pallas_call(
        second_turn_kernel if made else first_turn_kernel,
        out_shape=(
            jax.ShapeDtypeStruct((blocks * rows, rows - 1), F32),
            jax.ShapeDtypeStruct((groups * blocks, LANES), F32),
        ),
        in_specs=[smem, smem, vmem, vmem, vmem] + [vmem] * len(made),
        out_specs=(vmem, vmem),
        input_output_aliases={5: 0, 6: 1} if made else {},
        compiler_params=pltpu.CompilerParams(vmem_limit_bytes=40 * 2**20),
        cost_estimate=pl.CostEstimate(
            flops=8_000_000_000, bytes_accessed=8_000_000, transcendentals=0
        ),
        name="own_gram_second" if made else "own_gram_first",
    )(turn, obs_count, obs_index, localization, record, *made)


def lower_gram_kernel(gram_in, w_ref, lower_ref, gram_ref):
    gram_ref[...] = gram_in[...]
    add_gram(lower_ref, w_ref, 0, gram_in.shape[0] // lower_ref.shape[0], gram_ref)


def lower_gram(own, w, lower):
    vmem = pl.BlockSpec(memory_space=pltpu.VMEM)
    return pl.pallas_call(
        lower_gram_kernel,
        out_shape=jax.ShapeDtypeStruct(own.shape, F32),
        in_specs=[vmem, vmem, vmem],
        out_specs=vmem,
        input_output_aliases={0: 0},
        compiler_params=pltpu.CompilerParams(vmem_limit_bytes=40 * 2**20),
        cost_estimate=pl.CostEstimate(
            flops=2_000_000_000, bytes_accessed=2_000_000, transcendentals=0
        ),
        name="lower_gram",
    )(own, w, lower)


def padded(x):
    return jnp.concatenate([x, jnp.zeros((x.shape[0], LANES - x.shape[1]), x.dtype)], axis=1)


def terms(x):
    upper = x.astype(BF16)
    return upper, (x - upper.astype(F32)).astype(BF16)


def right_terms(x):
    upper, lower = terms(x)
    rest = jnp.zeros((LANES - x.shape[0], LANES), BF16)
    return (
        jnp.concatenate([upper, rest, upper, rest], axis=0),
        jnp.concatenate([lower, rest], axis=0),
    )


def multiply(x, right):
    upper, lower = terms(x)
    return jnp.dot(
        jnp.concatenate([upper, lower], axis=1), right[0], preferred_element_type=F32
    ) + jnp.dot(upper, right[1], preferred_element_type=F32)


def solve_blocks(informations, innovations):
    members = informations[0].shape[0]
    row_at = lax.broadcasted_iota(jnp.int32, (members, LANES), 0)
    column_at = lax.broadcasted_iota(jnp.int32, (members, LANES), 1)
    eye = (row_at == column_at).astype(F32)
    s, z, t, squares = [], [], [], []
    for gram, innovation in zip(informations, innovations):
        information = padded(gram) + (members - 1.0) * eye
        square = jnp.sum(information * information, axis=1, keepdims=True)
        square = jnp.sum(square, axis=0, keepdims=True)
        squares.append(square)
        s.append(information * lax.rsqrt(square))
        t.append(jnp.broadcast_to(padded(innovation), (8, LANES)))
        z.append(None)
    for sweep in range(NS_ITERS):
        final = sweep == NS_ITERS - 1
        rights = [right_terms(x) for x in s]
        for i in range(len(s)):
            lefts = ([] if final else [s[i]]) + ([z[i]] if sweep else []) + [t[i]]
            product = multiply(jnp.concatenate(lefts, axis=0), rights[i])
            at = 0 if final else members
            if sweep:
                z[i] = 1.5 * z[i] - 0.5 * product[at : at + members]
            else:
                z[i] = 1.5 * eye - 0.5 * s[i]
            if not final:
                s[i] = 1.5 * s[i] - 0.5 * product[:members]
            t[i] = 1.5 * t[i] - 0.5 * product[-8:]
        for i in range(len(s)):
            lefts = ([] if final else [s[i]]) + [t[i]]
            product = multiply(jnp.concatenate(lefts, axis=0), rights[i])
            if not final:
                s[i] = 1.5 * s[i] - 0.5 * product[:members]
            t[i] = 1.5 * t[i] - 0.5 * product[-8:]
    solved = []
    for square, z_i, t_i in zip(squares, z, t):
        inverse = lax.rsqrt(square)
        spread = (math.sqrt(members - 1.0) * jnp.sqrt(inverse)) * z_i[:, :members]
        solved.append(spread + inverse * t_i[:1, :members])
    return solved, eye[:, :members]


def finish_kernel(
    count_ref, own_ref, w_ref, upper_ref, background_ref, mean_ref, out_ref, gram_ref
):
    step = pl.program_id(0)
    blocks = count_ref.shape[0]
    members = background_ref.shape[1]

    @pl.when(step == 0)
    def _():
        gram_ref[...] = own_ref[...]
        groups = w_ref.shape[0] // blocks
        add_gram(upper_ref, w_ref, groups - HALO // LANES, blocks, gram_ref)

    informations, innovations = [], []
    for i in range(solve_batch):
        b = step * solve_batch + i
        informations.append(gram_ref[pl.ds(pl.multiple_of(b * members, members), members), :])
        innovations.append(gram_ref[pl.ds(blocks * members + b, 1), :])
    solved, eye = solve_blocks(informations, innovations)
    for i in range(solve_batch):
        b = step * solve_batch + i
        weights = jnp.where(count_ref[b] > 0, solved[i], eye).astype(BF16)
        mixed = jnp.dot(weights, background_ref[i], preferred_element_type=F32)
        out_ref[i] = (mean_ref[pl.ds(b, 1), :] + mixed).astype(BF16)


def finish(obs_count, own, w, upper, background, background_mean):
    blocks, members, cells = background.shape

    def whole(x):
        return pl.BlockSpec(x.shape, lambda i: (0,) * x.ndim)

    states = pl.BlockSpec((solve_batch, members, cells), lambda i: (i, 0, 0))
    return pl.pallas_call(
        finish_kernel,
        grid=(blocks // solve_batch,),
        out_shape=jax.ShapeDtypeStruct(background.shape, BF16),
        in_specs=[
            pl.BlockSpec(memory_space=pltpu.SMEM),
            whole(own),
            whole(w),
            whole(upper),
            states,
            whole(background_mean),
        ],
        out_specs=states,
        scratch_shapes=[pltpu.VMEM(own.shape, F32)],
        compiler_params=pltpu.CompilerParams(vmem_limit_bytes=40 * 2**20),
        name="finish",
    )(obs_count, own, w, upper, background, background_mean)


def on_device(observations, obs_index, obs_count, localization, background, background_mean):
    count = lax.axis_size("region")
    up = [(i, (i + 1) % count) for i in range(count)]
    down = [(j, i) for i, j in up]
    own_columns = observations.shape[1]
    place = lax.axis_index("region")
    turn = jnp.minimum(place % RUN, 1).astype(jnp.int32)[None]
    given = (turn, obs_count, obs_index, localization, observations)
    lower = lax.ppermute(observations[:, own_columns - HALO :], "region", up)
    made = own_gram(*given)
    first, *made = lax.optimization_barrier((observations[:, :HALO], *made))
    upper = lax.ppermute(first, "region", down)
    own, w = own_gram(*given, made)
    own = lower_gram(own, w, lower)
    return finish(obs_count, own, w, upper, background, background_mean)


def solution(mesh):
    return jax.shard_map(
        on_device,
        mesh=mesh,
        in_specs=(
            P(None, ("region", "group")),
            P(("region", "group"), None),
            P(("region", "group")),
            P(("region", "group"), None),
            P(("region", "group"), None, None),
            P(("region", "group"), None),
        ),
        out_specs=P(("region", "group"), None, None),
        check_vma=False,
    )
```

```python
import functools
import math

import jax
import jax.numpy as jnp
from jax import lax
from jax.experimental import pallas as pl
from jax.experimental.pallas import tpu as pltpu
from jax.sharding import PartitionSpec as P

HALO = 2048
NS_ITERS = 6
RUN = 8
LANES = 128
BF16 = jnp.bfloat16
F32 = jnp.float32
NT = (((1,), (1,)), ((), ()))

hist_unroll = 2
gram_chunk = 8


def histogram(block, count_ref, index_ref, factor_ref, w_ref):
    blocks, p_most = index_ref.shape
    groups = w_ref.shape[0] // blocks
    index = index_ref[pl.ds(block, 1), :]
    factor = factor_ref[pl.ds(block, 1), :]
    place = lax.broadcasted_iota(jnp.int32, (1, p_most), 1)
    factor = jnp.where(place < count_ref[block], factor, 0.0)
    hi = lax.shift_right_logical(index, 7)
    lo = lax.bitwise_and(index, LANES - 1)
    hi_at = lax.broadcasted_iota(jnp.int32, (groups, p_most), 0)
    lo_at = lax.broadcasted_iota(jnp.int32, (LANES, p_most), 0)
    hi_hot = jnp.where(hi_at == hi, factor, 0.0).astype(BF16)
    lo_hot = jnp.where(lo_at == lo, 1.0, 0.0).astype(BF16)
    summed = lax.dot_general(hi_hot, lo_hot, NT, preferred_element_type=F32)
    w_ref[pl.ds(block, groups, stride=blocks), :] = summed


def gram_part(record, w_ref, first, blocks):
    members = record.shape[0] - 1
    pieces = []
    for j in range(record.shape[1] // LANES):
        columns = slice(j * LANES, (j + 1) * LANES)
        perturbations = record[:members, columns]
        innovation = record[members:, columns].astype(F32)
        w = w_ref[pl.ds(pl.multiple_of((first + j) * blocks, blocks), blocks), :]
        rows = []
        for b in range(blocks):
            w_b = jnp.broadcast_to(w[b : b + 1, :], (16, LANES)).astype(BF16)
            rows.append(perturbations * jnp.concatenate([w_b] * (members // 16), axis=0))
        rows.append(w.astype(BF16) * jnp.broadcast_to(innovation, (blocks, LANES)).astype(BF16))
        pieces.append(jnp.concatenate(rows, axis=0))
    weighted = jnp.concatenate(pieces, axis=1)
    return lax.dot_general(weighted, record[:members], NT, preferred_element_type=F32)


def add_gram(record_ref, w_ref, first, blocks, sum_ref):
    width = gram_chunk * LANES

    def step(c, carry):
        record = record_ref[:, pl.ds(pl.multiple_of(c * width, width), width)]
        sum_ref[...] += gram_part(record, w_ref, first + c * gram_chunk, blocks)
        return carry

    lax.fori_loop(0, record_ref.shape[1] // width, step, 0)


def own_gram_body(count_ref, index_ref, factor_ref, record_ref, gram_ref, w_ref):
    blocks = index_ref.shape[0]

    def step(i, carry):
        for j in range(hist_unroll):
            histogram(i * hist_unroll + j, count_ref, index_ref, factor_ref, w_ref)
        return carry

    lax.fori_loop(0, blocks // hist_unroll, step, 0)
    gram_ref[...] = jnp.zeros_like(gram_ref)
    add_gram(record_ref, w_ref, HALO // LANES, blocks, gram_ref)


def first_turn_kernel(turn_ref, *refs):
    @pl.when(turn_ref[0] == 0)
    def _():
        own_gram_body(*refs)


def second_turn_kernel(turn_ref, count, index, factor, record, gram_in, w_in, gram_ref, w_ref):
    del gram_in, w_in

    @pl.when(turn_ref[0] != 0)
    def _():
        own_gram_body(count, index, factor, record, gram_ref, w_ref)


def own_gram(turn, obs_count, obs_index, localization, record, made=()):
    blocks, p_most = obs_index.shape
    rows, columns = record.shape
    groups = (columns + 2 * HALO) // LANES
    smem = pl.BlockSpec(memory_space=pltpu.SMEM)
    vmem = pl.BlockSpec(memory_space=pltpu.VMEM)
    return pl.pallas_call(
        second_turn_kernel if made else first_turn_kernel,
        out_shape=(
            jax.ShapeDtypeStruct((blocks * rows, rows - 1), F32),
            jax.ShapeDtypeStruct((groups * blocks, LANES), F32),
        ),
        in_specs=[smem, smem, vmem, vmem, vmem] + [vmem] * len(made),
        out_specs=(vmem, vmem),
        input_output_aliases={5: 0, 6: 1} if made else {},
        compiler_params=pltpu.CompilerParams(vmem_limit_bytes=40 * 2**20),
        cost_estimate=pl.CostEstimate(
            flops=8_000_000_000, bytes_accessed=8_000_000, transcendentals=0
        ),
        name="own_gram_second" if made else "own_gram_first",
    )(turn, obs_count, obs_index, localization, record, *made)


def lower_gram_kernel(gram_in, w_ref, lower_ref, gram_ref):
    gram_ref[...] = gram_in[...]
    add_gram(lower_ref, w_ref, 0, gram_in.shape[0] // lower_ref.shape[0], gram_ref)


def lower_gram(own, w, lower):
    vmem = pl.BlockSpec(memory_space=pltpu.VMEM)
    return pl.pallas_call(
        lower_gram_kernel,
        out_shape=jax.ShapeDtypeStruct(own.shape, F32),
        in_specs=[vmem, vmem, vmem],
        out_specs=vmem,
        input_output_aliases={0: 0},
        compiler_params=pltpu.CompilerParams(vmem_limit_bytes=40 * 2**20),
        cost_estimate=pl.CostEstimate(
            flops=2_000_000_000, bytes_accessed=2_000_000, transcendentals=0
        ),
        name="lower_gram",
    )(own, w, lower)


def padded(x):
    return jnp.concatenate([x, jnp.zeros((x.shape[0], LANES - x.shape[1]), x.dtype)], axis=1)


def terms(x):
    upper = x.astype(BF16)
    return upper, (x - upper.astype(F32)).astype(BF16)


def right_terms(x):
    both = jnp.concatenate(terms(x), axis=1)
    half = jnp.concatenate([both, jnp.zeros((LANES - x.shape[0], 2 * LANES), BF16)], axis=0)
    return jnp.concatenate([half, half], axis=0)


def multiply(x, right):
    product = jnp.dot(jnp.concatenate(terms(x), axis=1), right, preferred_element_type=F32)
    return product[:, :LANES] + product[:, LANES:]


def solve_blocks(informations, innovations):
    members = informations[0].shape[0]
    row_at = lax.broadcasted_iota(jnp.int32, (members, LANES), 0)
    column_at = lax.broadcasted_iota(jnp.int32, (members, LANES), 1)
    eye = (row_at == column_at).astype(F32)
    s, z, t, squares = [], [], [], []
    for gram, innovation in zip(informations, innovations):
        information = padded(gram) + (members - 1.0) * eye
        square = jnp.sum(information * information, axis=1, keepdims=True)
        square = jnp.sum(square, axis=0, keepdims=True)
        squares.append(square)
        s.append(information * lax.rsqrt(square))
        t.append(jnp.broadcast_to(padded(innovation), (8, LANES)))
        z.append(None)
    for sweep in range(NS_ITERS):
        final = sweep == NS_ITERS - 1
        rights = [right_terms(x) for x in s]
        for i in range(len(s)):
            lefts = ([] if final else [s[i]]) + ([z[i]] if sweep else []) + [t[i]]
            product = multiply(jnp.concatenate(lefts, axis=0), rights[i])
            at = 0 if final else members
            if sweep:
                z[i] = 1.5 * z[i] - 0.5 * product[at : at + members]
            else:
                z[i] = 1.5 * eye - 0.5 * s[i]
            if not final:
                s[i] = 1.5 * s[i] - 0.5 * product[:members]
            t[i] = 1.5 * t[i] - 0.5 * product[-8:]
        for i in range(len(s)):
            lefts = ([] if final else [s[i]]) + [t[i]]
            product = multiply(jnp.concatenate(lefts, axis=0), rights[i])
            if not final:
                s[i] = 1.5 * s[i] - 0.5 * product[:members]
            t[i] = 1.5 * t[i] - 0.5 * product[-8:]
    solved = []
    for square, z_i, t_i in zip(squares, z, t):
        inverse = lax.rsqrt(square)
        spread = (math.sqrt(members - 1.0) * jnp.sqrt(inverse)) * z_i[:, :members]
        solved.append(spread + inverse * t_i[:1, :members])
    return solved, eye[:, :members]


def finish_kernel(
    count_ref,
    own_ref,
    w_ref,
    upper_ref,
    background_ref,
    mean_ref,
    out_ref,
    gram_ref,
    made_ref,
    sems,
):
    blocks, members, _ = background_ref.shape
    groups = w_ref.shape[0] // blocks
    gram_ref[...] = own_ref[...]
    add_gram(upper_ref, w_ref, groups - HALO // LANES, blocks, gram_ref)
    informations = [gram_ref[b * members : (b + 1) * members, :] for b in range(blocks)]
    at = blocks * members
    innovations = [gram_ref[at + b : at + b + 1, :] for b in range(blocks)]
    solved, eye = solve_blocks(informations, innovations)
    copies = []
    for b in range(blocks):
        weights = jnp.where(count_ref[b] > 0, solved[b], eye).astype(BF16)
        mixed = jnp.dot(weights, background_ref[b], preferred_element_type=F32)
        made_ref[b] = (mean_ref[b : b + 1, :] + mixed).astype(BF16)
        copies.append(pltpu.make_async_copy(made_ref.at[b], out_ref.at[b], sems.at[b]))
        copies[b].start()
    for copy in copies:
        copy.wait()


def finish(obs_count, own, w, upper, background, background_mean):
    blocks = background.shape[0]
    vmem = pl.BlockSpec(memory_space=pltpu.VMEM)
    return pl.pallas_call(
        finish_kernel,
        out_shape=jax.ShapeDtypeStruct(background.shape, BF16),
        in_specs=[pl.BlockSpec(memory_space=pltpu.SMEM)] + [vmem] * 5,
        out_specs=pl.BlockSpec(memory_space=pl.ANY),
        scratch_shapes=[
            pltpu.VMEM(own.shape, F32),
            pltpu.VMEM(background.shape, BF16),
            pltpu.SemaphoreType.DMA((blocks,)),
        ],
        compiler_params=pltpu.CompilerParams(vmem_limit_bytes=40 * 2**20),
        name="finish",
    )(obs_count, own, w, upper, background, background_mean)


def on_device(observations, obs_index, obs_count, localization, background, background_mean):
    count = lax.axis_size("region")
    up = [(i, (i + 1) % count) for i in range(count)]
    down = [(j, i) for i, j in up]
    own_columns = observations.shape[1]
    place = lax.axis_index("region")
    turn = jnp.minimum(place % RUN // 2, 1).astype(jnp.int32)[None]
    given = (turn, obs_count, obs_index, localization, observations)
    lower = lax.ppermute(observations[:, own_columns - HALO :], "region", up)
    made = own_gram(*given)
    first, *made = lax.optimization_barrier((observations[:, :HALO], *made))
    upper = lax.ppermute(first, "region", down)
    own, w = own_gram(*given, made)
    own = lower_gram(own, w, lower)
    return finish(obs_count, own, w, upper, background, background_mean)


def solution(mesh):
    return jax.shard_map(
        on_device,
        mesh=mesh,
        in_specs=(
            P(None, ("region", "group")),
            P(("region", "group"), None),
            P(("region", "group")),
            P(("region", "group"), None),
            P(("region", "group"), None, None),
            P(("region", "group"), None),
        ),
        out_specs=P(("region", "group"), None, None),
        check_vma=False,
    )
```

```python
import functools
import math

import jax
import jax.numpy as jnp
from jax import lax
from jax.experimental import pallas as pl
from jax.experimental.pallas import tpu as pltpu
from jax.sharding import PartitionSpec as P

HALO = 2048
NS_ITERS = 6
RUN = 8
LANES = 128
BF16 = jnp.bfloat16
F32 = jnp.float32
NT = (((1,), (1,)), ((), ()))

hist_unroll = 8
gram_chunk = 8


def histogram(block, count_ref, index_ref, factor_ref, w_ref):
    blocks, p_most = index_ref.shape
    groups = w_ref.shape[0] // blocks
    index = index_ref[pl.ds(block, 1), :]
    factor = factor_ref[pl.ds(block, 1), :]
    place = lax.broadcasted_iota(jnp.int32, (1, p_most), 1)
    factor = jnp.where(place < count_ref[block], factor, 0.0)
    hi = lax.shift_right_logical(index, 7)
    lo = lax.bitwise_and(index, LANES - 1)
    hi_at = lax.broadcasted_iota(jnp.int32, (groups, p_most), 0)
    lo_at = lax.broadcasted_iota(jnp.int32, (LANES, p_most), 0)
    hi_hot = jnp.where(hi_at == hi, factor, 0.0).astype(BF16)
    lo_hot = jnp.where(lo_at == lo, 1.0, 0.0).astype(BF16)
    summed = lax.dot_general(lo_hot, hi_hot, NT, preferred_element_type=F32)
    w_ref[pl.ds(block, groups, stride=blocks), :] = summed.T


def gram_part(record, w_ref, first, blocks):
    members = record.shape[0] - 1
    pieces = []
    for j in range(record.shape[1] // LANES):
        columns = slice(j * LANES, (j + 1) * LANES)
        perturbations = record[:members, columns]
        innovation = record[members:, columns].astype(F32)
        w = w_ref[pl.ds(pl.multiple_of((first + j) * blocks, blocks), blocks), :]
        rows = []
        for b in range(blocks):
            w_b = jnp.broadcast_to(w[b : b + 1, :], (16, LANES)).astype(BF16)
            rows.append(perturbations * jnp.concatenate([w_b] * (members // 16), axis=0))
        rows.append(w.astype(BF16) * jnp.broadcast_to(innovation, (blocks, LANES)).astype(BF16))
        pieces.append(jnp.concatenate(rows, axis=0))
    weighted = jnp.concatenate(pieces, axis=1)
    return lax.dot_general(weighted, record[:members], NT, preferred_element_type=F32)


def add_gram(record_ref, w_ref, first, blocks, sum_ref):
    width = gram_chunk * LANES

    def step(c, carry):
        record = record_ref[:, pl.ds(pl.multiple_of(c * width, width), width)]
        sum_ref[...] += gram_part(record, w_ref, first + c * gram_chunk, blocks)
        return carry

    lax.fori_loop(0, record_ref.shape[1] // width, step, 0)


def early():
    return lax.axis_index("region") % RUN < 2


def own_gram_body(
    count_in, index_ref, factor_ref, record_ref, gram_ref, w_ref, active_ref, count_ref, sem
):
    copy = pltpu.make_async_copy(count_in, count_ref, sem)
    copy.start()
    copy.wait()
    blocks = index_ref.shape[0]

    def step(i, carry):
        for j in range(hist_unroll):
            histogram(i * hist_unroll + j, count_ref, index_ref, factor_ref, w_ref)
        return carry

    lax.fori_loop(0, blocks // hist_unroll, step, 0)
    for b in range(blocks):
        row = jnp.full((1, LANES), jnp.minimum(count_ref[b], 1), jnp.int32)
        active_ref[b : b + 1, :] = row.astype(F32)
    gram_ref[...] = jnp.zeros_like(gram_ref)
    add_gram(record_ref, w_ref, HALO // LANES, blocks, gram_ref)


def first_turn_kernel(*refs):
    @pl.when(early())
    def _():
        own_gram_body(*refs)


def second_turn_kernel(count, index, factor, record, gram_in, w_in, active_in, *made):
    del gram_in, w_in, active_in

    @pl.when(jnp.logical_not(early()))
    def _():
        own_gram_body(count, index, factor, record, *made)


def own_gram(obs_count, obs_index, localization, record, made=()):
    blocks = obs_index.shape[0]
    rows, columns = record.shape
    groups = (columns + 2 * HALO) // LANES
    vmem = pl.BlockSpec(memory_space=pltpu.VMEM)
    return pl.pallas_call(
        second_turn_kernel if made else first_turn_kernel,
        out_shape=(
            jax.ShapeDtypeStruct((blocks * rows, rows - 1), F32),
            jax.ShapeDtypeStruct((groups * blocks, LANES), F32),
            jax.ShapeDtypeStruct((blocks, LANES), F32),
        ),
        in_specs=[vmem] * (4 + len(made)),
        out_specs=(vmem,) * 3,
        scratch_shapes=[pltpu.SMEM((blocks,), jnp.int32), pltpu.SemaphoreType.DMA],
        input_output_aliases={4: 0, 5: 1, 6: 2} if made else {},
        compiler_params=pltpu.CompilerParams(vmem_limit_bytes=40 * 2**20),
        cost_estimate=pl.CostEstimate(
            flops=8_000_000_000, bytes_accessed=8_000_000, transcendentals=0
        ),
        name="own_gram_second" if made else "own_gram_first",
    )(obs_count, obs_index, localization, record, *made)


def lower_gram_kernel(gram_in, w_ref, lower_ref, gram_ref):
    gram_ref[...] = gram_in[...]
    add_gram(lower_ref, w_ref, 0, gram_in.shape[0] // lower_ref.shape[0], gram_ref)


def lower_gram(own, w, lower):
    vmem = pl.BlockSpec(memory_space=pltpu.VMEM)
    return pl.pallas_call(
        lower_gram_kernel,
        out_shape=jax.ShapeDtypeStruct(own.shape, F32),
        in_specs=[vmem, vmem, vmem],
        out_specs=vmem,
        input_output_aliases={0: 0},
        compiler_params=pltpu.CompilerParams(vmem_limit_bytes=40 * 2**20),
        cost_estimate=pl.CostEstimate(
            flops=2_000_000_000, bytes_accessed=2_000_000, transcendentals=0
        ),
        name="lower_gram",
    )(own, w, lower)


def padded(x):
    return jnp.concatenate([x, jnp.zeros((x.shape[0], LANES - x.shape[1]), x.dtype)], axis=1)


def terms(x):
    upper = x.astype(BF16)
    return upper, (x - upper.astype(F32)).astype(BF16)


def right_terms(x):
    both = jnp.concatenate(terms(x), axis=1)
    half = jnp.concatenate([both, jnp.zeros((LANES - x.shape[0], 2 * LANES), BF16)], axis=0)
    return jnp.concatenate([half, half], axis=0)


def multiply(x, right):
    product = jnp.dot(jnp.concatenate(terms(x), axis=1), right, preferred_element_type=F32)
    return product[:, :LANES] + product[:, LANES:]


def solve_blocks(informations, innovations):
    members = informations[0].shape[0]
    row_at = lax.broadcasted_iota(jnp.int32, (members, LANES), 0)
    column_at = lax.broadcasted_iota(jnp.int32, (members, LANES), 1)
    eye = (row_at == column_at).astype(F32)
    s, z, t, squares = [], [], [], []
    for gram, innovation in zip(informations, innovations):
        information = padded(gram) + (members - 1.0) * eye
        square = jnp.sum(information * information, axis=1, keepdims=True)
        square = jnp.sum(square, axis=0, keepdims=True)
        squares.append(square)
        s.append(information * lax.rsqrt(square))
        t.append(jnp.broadcast_to(padded(innovation), (8, LANES)))
        z.append(None)
    for sweep in range(NS_ITERS):
        final = sweep == NS_ITERS - 1
        rights = [right_terms(x) for x in s]
        for i in range(len(s)):
            lefts = ([] if final else [s[i]]) + ([z[i]] if sweep else []) + [t[i]]
            product = multiply(jnp.concatenate(lefts, axis=0), rights[i])
            at = 0 if final else members
            if sweep:
                z[i] = 1.5 * z[i] - 0.5 * product[at : at + members]
            else:
                z[i] = 1.5 * eye - 0.5 * s[i]
            if not final:
                s[i] = 1.5 * s[i] - 0.5 * product[:members]
            t[i] = 1.5 * t[i] - 0.5 * product[-8:]
        for i in range(len(s)):
            lefts = ([] if final else [s[i]]) + [t[i]]
            product = multiply(jnp.concatenate(lefts, axis=0), rights[i])
            if not final:
                s[i] = 1.5 * s[i] - 0.5 * product[:members]
            t[i] = 1.5 * t[i] - 0.5 * product[-8:]
    solved = []
    for square, z_i, t_i in zip(squares, z, t):
        inverse = lax.rsqrt(square)
        spread = (math.sqrt(members - 1.0) * jnp.sqrt(inverse)) * z_i[:, :members]
        solved.append(spread + inverse * t_i[:1, :members])
    return solved, eye[:, :members]


def finish_kernel(
    active_ref,
    own_ref,
    w_ref,
    upper_ref,
    background_ref,
    mean_ref,
    out_ref,
    gram_ref,
    made_ref,
    sems,
):
    blocks, members, _ = background_ref.shape
    groups = w_ref.shape[0] // blocks
    gram_ref[...] = own_ref[...]
    add_gram(upper_ref, w_ref, groups - HALO // LANES, blocks, gram_ref)
    informations = [gram_ref[b * members : (b + 1) * members, :] for b in range(blocks)]
    at = blocks * members
    innovations = [gram_ref[at + b : at + b + 1, :] for b in range(blocks)]
    solved, eye = solve_blocks(informations, innovations)
    copies = []
    for b in range(blocks):
        weights = jnp.where(active_ref[b : b + 1, :members] > 0.5, solved[b], eye).astype(BF16)
        mixed = jnp.dot(weights, background_ref[b], preferred_element_type=F32)
        made_ref[b] = (mean_ref[b : b + 1, :] + mixed).astype(BF16)
        copies.append(pltpu.make_async_copy(made_ref.at[b], out_ref.at[b], sems.at[b]))
        copies[b].start()
    for copy in copies:
        copy.wait()


def finish(active, own, w, upper, background, background_mean):
    blocks = background.shape[0]
    vmem = pl.BlockSpec(memory_space=pltpu.VMEM)
    return pl.pallas_call(
        finish_kernel,
        out_shape=jax.ShapeDtypeStruct(background.shape, BF16),
        in_specs=[vmem] * 6,
        out_specs=pl.BlockSpec(memory_space=pl.ANY),
        scratch_shapes=[
            pltpu.VMEM(own.shape, F32),
            pltpu.VMEM(background.shape, BF16),
            pltpu.SemaphoreType.DMA((blocks,)),
        ],
        compiler_params=pltpu.CompilerParams(vmem_limit_bytes=40 * 2**20),
        name="finish",
    )(active, own, w, upper, background, background_mean)


def on_device(observations, obs_index, obs_count, localization, background, background_mean):
    count = lax.axis_size("region")
    up = [(i, (i + 1) % count) for i in range(count)]
    down = [(j, i) for i, j in up]
    own_columns = observations.shape[1]
    given = (obs_count, obs_index, localization, observations)
    lower = lax.ppermute(observations[:, own_columns - HALO :], "region", up)
    made = own_gram(*given)
    below, *made = lax.optimization_barrier((observations[:, :HALO], *made))
    upper = lax.ppermute(below, "region", down)
    own, w, active = own_gram(*given, made)
    own = lower_gram(own, w, lower)
    return finish(active, own, w, upper, background, background_mean)


def solution(mesh):
    return jax.shard_map(
        on_device,
        mesh=mesh,
        in_specs=(
            P(None, ("region", "group")),
            P(("region", "group"), None),
            P(("region", "group")),
            P(("region", "group"), None),
            P(("region", "group"), None, None),
            P(("region", "group"), None),
        ),
        out_specs=P(("region", "group"), None, None),
        check_vma=False,
    )
```

```python
import functools
import math

import jax
import jax.numpy as jnp
from jax import lax
from jax.experimental import pallas as pl
from jax.experimental.pallas import tpu as pltpu
from jax.sharding import PartitionSpec as P

HALO = 2048
NS_ITERS = 6
RUN = 8
LANES = 128
BF16 = jnp.bfloat16
F32 = jnp.float32
NT = (((1,), (1,)), ((), ()))

hist_unroll = 8
gram_chunk = 8


def histogram(block, count_ref, index_ref, factor_ref, w_ref):
    blocks, p_most = index_ref.shape
    groups = w_ref.shape[0] // blocks
    index = index_ref[pl.ds(block, 1), :]
    factor = factor_ref[pl.ds(block, 1), :]
    place = lax.broadcasted_iota(jnp.int32, (1, p_most), 1)
    factor = jnp.where(place < count_ref[block], factor, 0.0)
    hi = lax.shift_right_logical(index, 7)
    lo = lax.bitwise_and(index, LANES - 1)
    hi_at = lax.broadcasted_iota(jnp.int32, (groups, p_most), 0)
    lo_at = lax.broadcasted_iota(jnp.int32, (LANES, p_most), 0)
    hi_hot = jnp.where(hi_at == hi, factor, 0.0).astype(BF16)
    lo_hot = jnp.where(lo_at == lo, 1.0, 0.0).astype(BF16)
    summed = lax.dot_general(lo_hot, hi_hot, NT, preferred_element_type=F32)
    w_ref[pl.ds(block, groups, stride=blocks), :] = summed.T


def gram_part(record, w_ref, first, blocks):
    members = record.shape[0] - 1
    pieces = []
    for j in range(record.shape[1] // LANES):
        columns = slice(j * LANES, (j + 1) * LANES)
        perturbations = record[:members, columns]
        innovation = record[members:, columns].astype(F32)
        w = w_ref[pl.ds(pl.multiple_of((first + j) * blocks, blocks), blocks), :]
        rows = []
        for b in range(blocks):
            w_b = jnp.broadcast_to(w[b : b + 1, :], (16, LANES)).astype(BF16)
            rows.append(perturbations * jnp.concatenate([w_b] * (members // 16), axis=0))
        rows.append(w.astype(BF16) * jnp.broadcast_to(innovation, (blocks, LANES)).astype(BF16))
        pieces.append(jnp.concatenate(rows, axis=0))
    weighted = jnp.concatenate(pieces, axis=1)
    return lax.dot_general(weighted, record[:members], NT, preferred_element_type=F32)


def add_gram(record_ref, w_ref, first, blocks, sum_ref):
    width = gram_chunk * LANES

    def step(c, carry):
        record = record_ref[:, pl.ds(pl.multiple_of(c * width, width), width)]
        sum_ref[...] += gram_part(record, w_ref, first + c * gram_chunk, blocks)
        return carry

    lax.fori_loop(0, record_ref.shape[1] // width, step, 0)


def early():
    return lax.axis_index("region") % RUN < 2


def own_gram_body(
    count_in, index_ref, factor_ref, record_ref, gram_ref, w_ref, active_ref, count_ref, sem
):
    copy = pltpu.make_async_copy(count_in, count_ref, sem)
    copy.start()
    copy.wait()
    blocks = index_ref.shape[0]

    def step(i, carry):
        for j in range(hist_unroll):
            histogram(i * hist_unroll + j, count_ref, index_ref, factor_ref, w_ref)
        return carry

    lax.fori_loop(0, blocks // hist_unroll, step, 0)
    for b in range(blocks):
        row = jnp.full((1, LANES), jnp.minimum(count_ref[b], 1), jnp.int32)
        active_ref[b : b + 1, :] = row.astype(F32)
    gram_ref[...] = jnp.zeros_like(gram_ref)
    add_gram(record_ref, w_ref, HALO // LANES, blocks, gram_ref)


def first_turn_kernel(*refs):
    @pl.when(early())
    def _():
        own_gram_body(*refs)


def second_turn_kernel(count, index, factor, record, gram_in, w_in, active_in, *made):
    del gram_in, w_in, active_in

    @pl.when(jnp.logical_not(early()))
    def _():
        own_gram_body(count, index, factor, record, *made)


def own_gram(obs_count, obs_index, localization, record, made=()):
    blocks = obs_index.shape[0]
    rows, columns = record.shape
    groups = (columns + 2 * HALO) // LANES
    vmem = pl.BlockSpec(memory_space=pltpu.VMEM)
    return pl.pallas_call(
        second_turn_kernel if made else first_turn_kernel,
        out_shape=(
            jax.ShapeDtypeStruct((blocks * rows, rows - 1), F32),
            jax.ShapeDtypeStruct((groups * blocks, LANES), F32),
            jax.ShapeDtypeStruct((blocks, LANES), F32),
        ),
        in_specs=[vmem] * (4 + len(made)),
        out_specs=(vmem,) * 3,
        scratch_shapes=[pltpu.SMEM((blocks,), jnp.int32), pltpu.SemaphoreType.DMA],
        input_output_aliases={4: 0, 5: 1, 6: 2} if made else {},
        compiler_params=pltpu.CompilerParams(vmem_limit_bytes=40 * 2**20),
        cost_estimate=pl.CostEstimate(
            flops=8_000_000_000, bytes_accessed=8_000_000, transcendentals=0
        ),
        name="own_gram_second" if made else "own_gram_first",
    )(obs_count, obs_index, localization, record, *made)


def lower_gram_kernel(gram_in, w_ref, lower_ref, gram_ref):
    blocks = gram_in.shape[0] // lower_ref.shape[0]
    gram_ref[...] = gram_in[...] + gram_part(lower_ref[...], w_ref, 0, blocks)


def lower_gram(own, w, lower):
    vmem = pl.BlockSpec(memory_space=pltpu.VMEM)
    return pl.pallas_call(
        lower_gram_kernel,
        out_shape=jax.ShapeDtypeStruct(own.shape, F32),
        in_specs=[vmem, vmem, vmem],
        out_specs=vmem,
        input_output_aliases={0: 0},
        compiler_params=pltpu.CompilerParams(vmem_limit_bytes=40 * 2**20),
        cost_estimate=pl.CostEstimate(
            flops=2_000_000_000, bytes_accessed=2_000_000, transcendentals=0
        ),
        name="lower_gram",
    )(own, w, lower)


def padded(x):
    return jnp.concatenate([x, jnp.zeros((x.shape[0], LANES - x.shape[1]), x.dtype)], axis=1)


def terms(x):
    upper = x.astype(BF16)
    return upper, (x - upper.astype(F32)).astype(BF16)


def right_terms(x):
    both = jnp.concatenate(terms(x), axis=1)
    half = jnp.concatenate([both, jnp.zeros((LANES - x.shape[0], 2 * LANES), BF16)], axis=0)
    return jnp.concatenate([half, half], axis=0)


def multiply(x, right):
    product = jnp.dot(jnp.concatenate(terms(x), axis=1), right, preferred_element_type=F32)
    return product[:, :LANES] + product[:, LANES:]


def solve_blocks(informations, innovations):
    members = informations[0].shape[0]
    row_at = lax.broadcasted_iota(jnp.int32, (members, LANES), 0)
    column_at = lax.broadcasted_iota(jnp.int32, (members, LANES), 1)
    eye = (row_at == column_at).astype(F32)
    s, z, t, squares = [], [], [], []
    for gram, innovation in zip(informations, innovations):
        information = padded(gram) + (members - 1.0) * eye
        square = jnp.sum(information * information, axis=1, keepdims=True)
        square = jnp.sum(square, axis=0, keepdims=True)
        squares.append(square)
        s.append(information * lax.rsqrt(square))
        t.append(jnp.broadcast_to(padded(innovation), (8, LANES)))
        z.append(None)
    for sweep in range(NS_ITERS):
        final = sweep == NS_ITERS - 1
        rights = [right_terms(x) for x in s]
        for i in range(len(s)):
            lefts = ([] if final else [s[i]]) + ([z[i]] if sweep else []) + [t[i]]
            product = multiply(jnp.concatenate(lefts, axis=0), rights[i])
            at = 0 if final else members
            if sweep:
                z[i] = 1.5 * z[i] - 0.5 * product[at : at + members]
            else:
                z[i] = 1.5 * eye - 0.5 * s[i]
            if not final:
                s[i] = 1.5 * s[i] - 0.5 * product[:members]
            t[i] = 1.5 * t[i] - 0.5 * product[-8:]
        for i in range(len(s)):
            lefts = ([] if final else [s[i]]) + [t[i]]
            product = multiply(jnp.concatenate(lefts, axis=0), rights[i])
            if not final:
                s[i] = 1.5 * s[i] - 0.5 * product[:members]
            t[i] = 1.5 * t[i] - 0.5 * product[-8:]
    solved = []
    for square, z_i, t_i in zip(squares, z, t):
        inverse = lax.rsqrt(square)
        spread = (math.sqrt(members - 1.0) * jnp.sqrt(inverse)) * z_i[:, :members]
        solved.append(spread + inverse * t_i[:1, :members])
    return solved, eye[:, :members]


def finish_kernel(
    active_ref,
    own_ref,
    w_ref,
    upper_ref,
    background_ref,
    mean_ref,
    out_ref,
    gram_ref,
    made_ref,
    sems,
):
    blocks, members, _ = background_ref.shape
    groups = w_ref.shape[0] // blocks
    upper = gram_part(upper_ref[...], w_ref, groups - HALO // LANES, blocks)
    gram_ref[...] = own_ref[...] + upper
    informations = [gram_ref[b * members : (b + 1) * members, :] for b in range(blocks)]
    at = blocks * members
    innovations = [gram_ref[at + b : at + b + 1, :] for b in range(blocks)]
    solved, eye = solve_blocks(informations, innovations)
    copies = []
    for b in range(blocks):
        weights = jnp.where(active_ref[b : b + 1, :members] > 0.5, solved[b], eye).astype(BF16)
        mixed = jnp.dot(weights, background_ref[b], preferred_element_type=F32)
        made_ref[b] = (mean_ref[b : b + 1, :] + mixed).astype(BF16)
        copies.append(pltpu.make_async_copy(made_ref.at[b], out_ref.at[b], sems.at[b]))
        copies[b].start()
    for copy in copies:
        copy.wait()


def finish(active, own, w, upper, background, background_mean):
    blocks = background.shape[0]
    vmem = pl.BlockSpec(memory_space=pltpu.VMEM)
    return pl.pallas_call(
        finish_kernel,
        out_shape=jax.ShapeDtypeStruct(background.shape, BF16),
        in_specs=[vmem] * 6,
        out_specs=pl.BlockSpec(memory_space=pl.ANY),
        scratch_shapes=[
            pltpu.VMEM(own.shape, F32),
            pltpu.VMEM(background.shape, BF16),
            pltpu.SemaphoreType.DMA((blocks,)),
        ],
        compiler_params=pltpu.CompilerParams(vmem_limit_bytes=40 * 2**20),
        name="finish",
    )(active, own, w, upper, background, background_mean)


def on_device(observations, obs_index, obs_count, localization, background, background_mean):
    count = lax.axis_size("region")
    up = [(i, (i + 1) % count) for i in range(count)]
    down = [(j, i) for i, j in up]
    own_columns = observations.shape[1]
    given = (obs_count, obs_index, localization, observations)
    lower = lax.ppermute(observations[:, own_columns - HALO :], "region", up)
    made = own_gram(*given)
    below, *made = lax.optimization_barrier((observations[:, :HALO], *made))
    upper = lax.ppermute(below, "region", down)
    own, w, active = own_gram(*given, made)
    own = lower_gram(own, w, lower)
    return finish(active, own, w, upper, background, background_mean)


def solution(mesh):
    return jax.shard_map(
        on_device,
        mesh=mesh,
        in_specs=(
            P(None, ("region", "group")),
            P(("region", "group"), None),
            P(("region", "group")),
            P(("region", "group"), None),
            P(("region", "group"), None, None),
            P(("region", "group"), None),
        ),
        out_specs=P(("region", "group"), None, None),
        check_vma=False,
    )
```
